32 devices in a mesh: seq: 8 (over z, x), head: 4 (over y, core).
Axes of the slice: x: 2, y: 2, z: 4, core: 2. Of those that a mesh axis runs over, the one named last changes fastest.
Arguments:
- query: bfloat16 [4096, 4096], P(('seq', 'head')), may hold values from -41 to 41
- keys: bfloat16 [131072, 1024], P('seq', 'head'), may hold values from -14 to 14
- values: bfloat16 [131072, 1024], P('seq', 'head'), may hold values from -6 to 6
- out_grad: bfloat16 [4096, 4096], P(('seq', 'head')), may hold values from -6 to 6
- span_pos: int32 [8], P('seq'), may hold values from 1 to 31, as said below
- selected: int32 [8, 4], P('seq'), may hold values from -1 to 254, as said below
Outputs:
- attn_out: bfloat16 [4096, 4096], P(('seq', 'head'))
- query_grad: bfloat16 [4096, 4096], P(('seq', 'head'))
- key_grad: bfloat16 [131072, 1024], P('seq', 'head')
- value_grad: bfloat16 [131072, 1024], P('seq', 'head')
The draws below stay inside these ranges and needn't reach their ends.
Inputs may be any that keep to these rules, and one draw needn't show every extreme that they name: `span_pos`: block index of the span's queries within its shard. `selected`: entry [s, j] is -1 if s < j; otherwise it indexes a block of shard s - j (blocks (s - j) * 32 onward), and for j = 0 one earlier than span s's own block s * 32 + span_pos[s].
All inputs are finite; a program needn't handle non-finite values.
Results may differ from the reference program's by a relative error of at most 0.029.
Values may be sent and summed in bfloat16 or wider, within the bound.
No kernel may reach another device: no remote copies, remote signals or barrier semaphores. Data moves between devices by JAX's collectives and lax.ppermute only.
A program may use at most 192 MiB of HBM per device.

```python
import jax
import jax.numpy as jnp
from jax import lax

HEADS = 32
KV_HEADS = 8
HEAD_DIM = 128
BLOCK = 512
TOPK = 4
SHARD = 16384
SEQ = 131072
QROWS = 4096
N_SEQ = 8


def pick_blocks(key):
    base_key = jax.random.fold_in(key, 7)
    pos_key, block_key = jax.random.split(base_key, 2)
    shard_blocks = SHARD // BLOCK
    span_block = jax.random.randint(pos_key, (N_SEQ,), 1, shard_blocks)
    device_ids = jnp.arange(N_SEQ)
    pick_ids = jnp.arange(TOPK)
    source = device_ids[:, None] - pick_ids[None, :]
    upper_limit = jnp.where(pick_ids[None, :] == 0, span_block[:, None], shard_blocks)
    within = jax.random.randint(block_key, (N_SEQ, TOPK), 0, 1 << 20) % upper_limit
    chosen = jnp.where(source >= 0, source * shard_blocks + within, -1)
    return (span_block.astype(jnp.int32), chosen.astype(jnp.int32))


def draw_span_pos(key, part):
    return pick_blocks(key)[0]


def draw_selected(key, part):
    return pick_blocks(key)[1]


def draw_keys(key, part):
    key_table = jnp.clip(jax.random.normal(jax.random.fold_in(key, 11), (N_SEQ * SHARD, KV_HEADS * HEAD_DIM), jnp.float32), -4.5, 4.5)
    return key_table.astype(jnp.bfloat16)


def draw_query(key, part):
    query_table = jnp.clip(jax.random.normal(jax.random.fold_in(key, 13), (N_SEQ * BLOCK, HEADS * HEAD_DIM), jnp.float32), -4.5, 4.5)
    return query_table.astype(jnp.bfloat16)


def shard_levels(rng, dims, cuts, least, high):
    def one(dim, blocks):
        draws = jax.random.uniform(jax.random.fold_in(jax.random.fold_in(rng, 6), dim), (blocks,), jnp.float32, least / len(cuts), high / len(cuts))
        return jnp.repeat(jnp.exp(draws), dims[dim] // blocks).reshape((-1,) + (1,) * (len(dims) - dim - 1))

    gain = one(*cuts[0])
    for cut in cuts[1:]:
        gain = gain * one(*cut)
    return gain


def centred(stream_key, dims, width, limit, cuts=(), kind=jnp.bfloat16):
    level = shard_levels(stream_key, dims, cuts, -0.22, 0.18) if cuts else 1.0
    result = jax.random.normal(stream_key, dims, jnp.float32) * width * level
    return jnp.minimum(jnp.maximum(result, -limit), limit).astype(kind)


def setup_inputs(seed: int = 0) -> dict:
    seeds = jax.random.split(jax.random.key(seed), 7)
    return {
        "query": draw_query(jax.random.fold_in(seeds[6], 71), 0),
        "keys": draw_keys(jax.random.fold_in(seeds[6], 71), 0),
        "values": centred(seeds[2], (SEQ, KV_HEADS * HEAD_DIM), 1.0, 6.0, ((0, 8), (1, 4))),
        "out_grad": centred(seeds[3], (QROWS, HEADS * HEAD_DIM), 1.0, 6.0, ((0, 32),)),
        "span_pos": draw_span_pos(jax.random.fold_in(seeds[6], 71), 0),
        "selected": draw_selected(jax.random.fold_in(seeds[6], 71), 0),
    }


masked_score = -1e30


def attend(query_rows, grad_rows, key_rows, value_rows, allowed, score_scale):
    query_float = query_rows.astype(jnp.float32)
    grad_float = grad_rows.astype(jnp.float32)
    key_float = key_rows.astype(jnp.float32)
    value_float = value_rows.astype(jnp.float32)
    scores = jnp.einsum("qhgd,khd->hgqk", query_float, key_float) * score_scale
    scores = jnp.where(allowed, scores, masked_score)
    row_max = jnp.max(scores, axis=-1, keepdims=True)
    exponent = jnp.exp(scores - row_max)
    weights = exponent / jnp.sum(exponent, axis=-1, keepdims=True)
    weights_low = weights.astype(jnp.bfloat16)
    weights_back = weights_low.astype(jnp.float32)
    attended = jnp.einsum("hgqk,khd->qhgd", weights_back, value_float).astype(jnp.bfloat16)
    row_delta = jnp.sum(grad_float * attended.astype(jnp.float32), axis=-1)
    weight_grad = jnp.einsum("qhgd,khd->hgqk", grad_float, value_float)
    score_grad = (weights * (weight_grad - jnp.transpose(row_delta, (1, 2, 0))[..., None])).astype(jnp.bfloat16)
    grad_back = score_grad.astype(jnp.float32)
    query_part = (jnp.einsum("hgqk,khd->qhgd", grad_back, key_float) * score_scale).astype(jnp.bfloat16)
    key_part = (jnp.einsum("hgqk,qhgd->khd", grad_back, query_float) * score_scale).astype(jnp.bfloat16)
    value_part = jnp.einsum("hgqk,qhgd->khd", weights_back, grad_float).astype(jnp.bfloat16)
    return attended, query_part, key_part, value_part


def reference(query, keys, values, out_grad, span_pos, selected):
    group_size = HEADS // KV_HEADS
    shard_blocks = SHARD // BLOCK
    feature_width = KV_HEADS * HEAD_DIM
    score_scale = HEAD_DIM ** -0.5
    key_total = jnp.zeros(keys.shape, jnp.float32)
    value_total = jnp.zeros(values.shape, jnp.float32)
    columns = jnp.arange((TOPK + 1) * BLOCK)
    query_pos = jnp.arange(BLOCK)
    slot_of = columns // BLOCK
    attended_all = []
    query_grads = []
    for shard_index in range(N_SEQ):
        chosen = selected[shard_index].astype(jnp.int32)
        usable = chosen >= 0
        own_block = shard_index * shard_blocks + span_pos[shard_index].astype(jnp.int32)
        starts = [jnp.maximum(chosen[pick_index], 0) * BLOCK for pick_index in range(TOPK)] + [own_block * BLOCK]
        key_rows = jnp.concatenate([lax.dynamic_slice_in_dim(keys, block_start, BLOCK, 0) for block_start in starts], 0)
        value_rows = jnp.concatenate([lax.dynamic_slice_in_dim(values, block_start, BLOCK, 0) for block_start in starts], 0)
        slot_ok = jnp.concatenate([usable, jnp.ones((1,), jnp.bool_)])[slot_of]
        allowed = jnp.where(slot_of[None, :] == TOPK, (columns % BLOCK)[None, :] <= query_pos[:, None], slot_ok[None, :])
        query_rows = query[shard_index * BLOCK:(shard_index + 1) * BLOCK].reshape(BLOCK, KV_HEADS, group_size, HEAD_DIM)
        grad_rows = out_grad[shard_index * BLOCK:(shard_index + 1) * BLOCK].reshape(BLOCK, KV_HEADS, group_size, HEAD_DIM)
        attended, query_part, key_part, value_part = attend(
            query_rows, grad_rows,
            key_rows.reshape(-1, KV_HEADS, HEAD_DIM), value_rows.reshape(-1, KV_HEADS, HEAD_DIM),
            allowed, score_scale)
        key_part = key_part.reshape(-1, feature_width).astype(jnp.float32)
        value_part = value_part.reshape(-1, feature_width).astype(jnp.float32)
        for pick_index, block_start in enumerate(starts):
            keep_piece = usable[pick_index] if pick_index < TOPK else jnp.ones((), jnp.bool_)
            key_piece = jnp.where(keep_piece, key_part[pick_index * BLOCK:(pick_index + 1) * BLOCK], 0.0)
            value_piece = jnp.where(keep_piece, value_part[pick_index * BLOCK:(pick_index + 1) * BLOCK], 0.0)
            key_total = lax.dynamic_update_slice_in_dim(
                key_total, lax.dynamic_slice_in_dim(key_total, block_start, BLOCK, 0) + key_piece, block_start, 0)
            value_total = lax.dynamic_update_slice_in_dim(
                value_total, lax.dynamic_slice_in_dim(value_total, block_start, BLOCK, 0) + value_piece, block_start, 0)
        attended_all.append(attended.reshape(BLOCK, HEADS * HEAD_DIM))
        query_grads.append(query_part.reshape(BLOCK, HEADS * HEAD_DIM))
    return (jnp.concatenate(attended_all, 0), jnp.concatenate(query_grads, 0),
            key_total.astype(jnp.bfloat16), value_total.astype(jnp.bfloat16))
```

```python
import functools
import math

import jax
import jax.numpy as jnp
from jax import lax
from jax.experimental import pallas as pl
from jax.experimental.pallas import tpu as pltpu
from jax.sharding import PartitionSpec as P

HEAD_DIM = 128
MASKED = -1e30
VMEM_LIMIT = 48 << 20

ROWS_ROWS = (((1,), (1,)), ((), ()))
ROWS_COLS = (((1,), (0,)), ((), ()))
HBM = pl.BlockSpec(memory_space=pl.ANY)
SMEM = pl.BlockSpec(memory_space=pltpu.SMEM)
VMEM = pl.BlockSpec(memory_space=pltpu.VMEM)


def shifted(value, axis, steps):
    count = lax.axis_size(axis)
    first, last = (max(0, -steps), min(count, count - steps))
    return lax.ppermute(value, axis, [(source, source + steps) for source in range(first, last)])


def flipped(value, axis, mask):
    count = lax.axis_size(axis)
    return lax.ppermute(value, axis, [(source, source ^ mask) for source in range(count)])


def dot(left, right, dims):
    return lax.dot_general(left, right, dims, preferred_element_type=jnp.float32)


def split_queries(query, out_grad, me, heads):
    rows, width = query.shape
    count = lax.axis_size("head")
    part = width // (count * heads)

    def kernel(me_ref, q_ref, g_ref, *outs):
        for head in range(heads):
            for r in range(count):
                start = pl.multiple_of((me_ref[0] ^ r) * heads * part + head * part, 128)
                outs[head * count + r][0] = q_ref[:, pl.ds(start, part)]
                outs[head * count + r][1] = g_ref[:, pl.ds(start, part)]

    flat = pl.pallas_call(
        kernel,
        in_specs=[SMEM, VMEM, VMEM],
        out_specs=[VMEM] * (heads * count),
        out_shape=[jax.ShapeDtypeStruct((2, rows, part), query.dtype)] * (heads * count),
        compiler_params=pltpu.CompilerParams(vmem_limit_bytes=VMEM_LIMIT),
        name="split_queries",
    )(me, query, out_grad)
    return [flat[head * count : (head + 1) * count] for head in range(heads)]


def gather_blocks(keys, values, wanted, seq_index, block_rows, heads):
    shard_blocks = keys.shape[0] // block_rows
    count = len(wanted)

    def kernel(seq_ref, *refs):
        entries = refs[:count]
        k_ref, v_ref = refs[count : count + 2]
        outs = refs[count + 2 : -1]
        sem = refs[-1]
        copies = []
        for head in range(heads):
            for d in range(count):
                local = entries[d][0, d + 1] - seq_ref[0] * shard_blocks
                local = jnp.clip(local, 0, shard_blocks - 1)
                rows = pl.ds(pl.multiple_of(local * block_rows, block_rows), block_rows)
                cols = pl.ds(head * HEAD_DIM, HEAD_DIM)
                for which, source in enumerate((k_ref, v_ref)):
                    slot = (head * count + d) * 2 + which
                    copies.append(
                        pltpu.make_async_copy(
                            source.at[rows, cols], outs[head * count + d].at[which], sem.at[slot]
                        )
                    )
        for copy in copies:
            copy.start()
        for copy in copies:
            copy.wait()

    flat = pl.pallas_call(
        kernel,
        in_specs=[SMEM] * (1 + count) + [HBM, HBM],
        out_specs=[VMEM] * (heads * count),
        out_shape=[jax.ShapeDtypeStruct((2, block_rows, HEAD_DIM), keys.dtype)] * (heads * count),
        scratch_shapes=[pltpu.SemaphoreType.DMA((heads * count * 2,))],
        compiler_params=pltpu.CompilerParams(vmem_limit_bytes=VMEM_LIMIT),
        name="gather_blocks",
    )(seq_index, *wanted, keys, values)
    return [flat[head * count : (head + 1) * count] for head in range(heads)]


def attend(me, chosen, span_pos, pieces, keys, values, arrived, head):
    count = len(pieces)
    rows = pieces[0].shape[1]
    group = pieces[0].shape[2] // HEAD_DIM
    block = count * rows
    picks = chosen.shape[1]
    slots = picks + 1
    shard_blocks = keys.shape[0] // block
    scale = HEAD_DIM**-0.5
    log2e = math.log2(math.e)
    fresh = 2 if head == 0 else 0
    clear_rows = math.gcd(keys.shape[0], 2048)
    clear_steps = keys.shape[0] // clear_rows
    clear_scratch = []
    if fresh:
        clear_scratch.append(pltpu.VMEM((clear_rows, keys.shape[1]), keys.dtype))
        clear_scratch.append(pltpu.SemaphoreType.DMA((fresh * clear_steps,)))

    def kernel(me_ref, chosen_ref, pos_ref, *refs):
        piece_refs, refs = refs[:count], refs[count:]
        first_k, first_v, own_k, own_v = refs[:4]
        refs = refs[4:]
        arrived_refs, refs = refs[: picks - 1], refs[picks - 1 :]
        out_refs, refs = refs[:count], refs[count:]
        grad_refs, refs = refs[:slots], refs[slots:]
        zero_refs, refs = refs[:fresh], refs[fresh:]
        s_ref, acc_k, acc_v, k_t, v_t = refs[:5]
        key_refs = [first_k] + [ref.at[0] for ref in arrived_refs] + [own_k]
        value_refs = [first_v] + [ref.at[1] for ref in arrived_refs] + [own_v]
        spans = [slice(slot * block, (slot + 1) * block) for slot in range(slots)]
        step = pl.program_id(0)
        clears = []
        if fresh:
            blank, blank_sem = refs[5:]
            for which, target in enumerate(zero_refs):
                for part in range(clear_steps):
                    place = target.at[pl.ds(part * clear_rows, clear_rows)]
                    slot = blank_sem.at[which * clear_steps + part]
                    clears.append(pltpu.make_async_copy(blank, place, slot))

        @pl.when(step == 0)
        def _():
            if fresh:
                blank[...] = jnp.zeros_like(blank)
            for clear in clears:
                clear.start()
            for slot in range(slots):
                k_t[:, spans[slot]] = key_refs[slot][...].T
                v_t[:, spans[slot]] = value_refs[slot][...].T

        q = jnp.concatenate([ref[0] for ref in piece_refs], 0)
        g = jnp.concatenate([ref[1] for ref in piece_refs], 0)
        top = jnp.full((1, block), MASKED, jnp.float32)
        for slot in range(slots):
            s = dot(key_refs[slot][...], q, ROWS_ROWS) * (scale * log2e)
            if slot == picks:
                key_pos = lax.broadcasted_iota(jnp.int32, (block, block), 0)
                column = lax.broadcasted_iota(jnp.int32, (block, block), 1)
                query_pos = ((column // rows) ^ me_ref[0]) * rows + column % rows
                s = jnp.where(key_pos <= query_pos, s, MASKED)
            else:
                s = jnp.where(chosen_ref[0, slot] >= 0, s, MASKED)
            s_ref[spans[slot]] = s
            top = jnp.maximum(top, jnp.max(s, axis=0, keepdims=True))
        total = jnp.zeros((1, block), jnp.float32)
        for slot in range(slots):
            e = jnp.exp2(s_ref[spans[slot]] - top)
            s_ref[spans[slot]] = e
            total = total + jnp.sum(e, axis=0, keepdims=True)
        inverse = 1.0 / total
        o_t = jnp.zeros((HEAD_DIM, block), jnp.float32)
        for slot in range(slots):
            w = s_ref[spans[slot]] * inverse
            s_ref[spans[slot]] = w
            low = w.astype(jnp.bfloat16)
            o_t = o_t + dot(v_t[:, spans[slot]], low, ROWS_COLS)
            before = jnp.where(step == 0, 0.0, acc_v[spans[slot]])
            acc_v[spans[slot]] = before + dot(low, g, ROWS_COLS)
        o_t = o_t.astype(jnp.bfloat16).astype(jnp.float32)
        delta = jnp.sum(g.T.astype(jnp.float32) * o_t, axis=0, keepdims=True)
        q_t = jnp.zeros((HEAD_DIM, block), jnp.float32)
        for slot in range(slots):
            w_grad = dot(value_refs[slot][...], g, ROWS_ROWS)
            s_grad = (s_ref[spans[slot]] * (w_grad - delta)).astype(jnp.bfloat16)
            q_t = q_t + dot(k_t[:, spans[slot]], s_grad, ROWS_COLS)
            before = jnp.where(step == 0, 0.0, acc_k[spans[slot]])
            acc_k[spans[slot]] = before + dot(s_grad, q, ROWS_COLS)
        o = o_t.T.astype(jnp.bfloat16)
        q_grad = (q_t * scale).T.astype(jnp.bfloat16)
        for r in range(count):
            out_refs[r][0] = o[r * rows : (r + 1) * rows]
            out_refs[r][1] = q_grad[r * rows : (r + 1) * rows]

        @pl.when(step == group - 1)
        def _():
            for slot in range(slots):
                grad_refs[slot][0] = (acc_k[spans[slot]] * scale).astype(jnp.bfloat16)
                grad_refs[slot][1] = acc_v[spans[slot]].astype(jnp.bfloat16)
            for clear in clears:
                clear.wait()

    def first_index(step, me, chosen, pos):
        return (jnp.maximum(lax.rem(chosen[0, 0], shard_blocks), 0), head)

    def own_index(step, me, chosen, pos):
        return (pos[0], head)

    def whole_index(step, me, chosen, pos):
        return (0, 0, 0)

    piece = pl.BlockSpec((2, rows, HEAD_DIM), lambda step, me, chosen, pos: (0, 0, step))
    pair = pl.BlockSpec((2, block, HEAD_DIM), whole_index)
    flops = 12 * block * slots * block * HEAD_DIM * group
    result = pl.pallas_call(
        kernel,
        grid_spec=pltpu.PrefetchScalarGridSpec(
            num_scalar_prefetch=3,
            grid=(group,),
            in_specs=[piece] * count
            + [pl.BlockSpec((block, HEAD_DIM), first_index)] * 2
            + [pl.BlockSpec((block, HEAD_DIM), own_index)] * 2
            + [pair] * (picks - 1),
            out_specs=[piece] * count + [pair] * slots + [HBM] * fresh,
            scratch_shapes=[
                pltpu.VMEM((slots * block, block), jnp.float32),
                pltpu.VMEM((slots * block, HEAD_DIM), jnp.float32),
                pltpu.VMEM((slots * block, HEAD_DIM), jnp.float32),
                pltpu.VMEM((HEAD_DIM, slots * block), jnp.bfloat16),
                pltpu.VMEM((HEAD_DIM, slots * block), jnp.bfloat16),
            ]
            + clear_scratch,
        ),
        out_shape=[jax.ShapeDtypeStruct(pieces[0].shape, jnp.bfloat16)] * count
        + [jax.ShapeDtypeStruct((2, block, HEAD_DIM), jnp.bfloat16)] * slots
        + [jax.ShapeDtypeStruct(keys.shape, keys.dtype)] * fresh,
        compiler_params=pltpu.CompilerParams(vmem_limit_bytes=VMEM_LIMIT),
        cost_estimate=pl.CostEstimate(
            flops=flops, bytes_accessed=8 << 20, transcendentals=block * block * slots * group
        ),
        name="attend",
    )(me, chosen, span_pos, *pieces, keys, values, keys, values, *arrived)
    return (result[:count], result[count : count + slots], result[count + slots :])


def finish(ids, chosen, span_pos, wanted, outs, contributions, buffers, shapes, head, heads):
    count = len(outs)
    rows, part = outs[0].shape[1:]
    slots = len(contributions)
    picks = slots - 1
    block = contributions[0].shape[1]
    fresh = len(shapes) - len(buffers)

    def kernel(ids_ref, chosen_ref, pos_ref, *refs):
        wanted_refs, refs = refs[: picks - 1], refs[picks - 1 :]
        out_refs, refs = refs[:count], refs[count:]
        given, refs = refs[:slots], refs[slots:]
        refs = refs[len(buffers) :]
        attn_ref, query_ref, key_ref, value_ref = refs[:4]
        sums, out_sem, grad_sem = refs[4:]
        seq, me = ids_ref[0], ids_ref[1]
        shard_blocks = key_ref.shape[0] // block
        copies = []
        for r in range(count):
            start = pl.multiple_of((me ^ r) * heads * part + head * part, 128)
            for which, target in enumerate((attn_ref, query_ref)):
                copies.append(
                    pltpu.make_async_copy(
                        out_refs[r].at[which],
                        target.at[:, pl.ds(start, part)],
                        out_sem.at[r * 2 + which],
                    )
                )
        for copy in copies:
            copy.start()
        targets = [jnp.where(chosen_ref[0, 0] >= 0, chosen_ref[0, 0] - seq * shard_blocks, -1)]
        for d in range(1, picks):
            above = seq + d < lax.axis_size("seq")
            local = wanted_refs[d - 1][0, d] - seq * shard_blocks
            targets.append(jnp.where(above, local, -1))
        targets.append(pos_ref[0])
        present = [(t >= 0) & (t < shard_blocks) for t in targets]
        same = {}
        for i in range(slots):
            for j in range(i + 1, slots):
                same[i, j] = present[i] & (targets[i] == targets[j])

        def moves(i, source):
            start = pl.multiple_of(jnp.clip(targets[i], 0, shard_blocks - 1) * block, block)
            place = (pl.ds(start, block), pl.ds(head * HEAD_DIM, HEAD_DIM))
            return [
                pltpu.make_async_copy(source.at[which], target.at[place], grad_sem.at[i * 2 + which])
                for which, target in enumerate((key_ref, value_ref))
            ]

        leads = []
        for i in range(slots):
            lead = present[i]
            for j in range(i):
                lead = lead & jnp.logical_not(same[j, i])
            shared = jnp.bool_(False)
            for j in range(i + 1, slots):
                shared = shared | same[i, j]
            leads.append(lead)

            @pl.when(lead & jnp.logical_not(shared))
            def _(i=i):
                for copy in moves(i, given[i]):
                    copy.start()

            @pl.when(lead & shared)
            def _(i=i):
                value = given[i][...].astype(jnp.float32)
                for j in range(i + 1, slots):
                    value = value + jnp.where(same[i, j], given[j][...].astype(jnp.float32), 0.0)
                sums[i] = value.astype(jnp.bfloat16)
                for copy in moves(i, sums.at[i]):
                    copy.start()

        for i in range(slots):

            @pl.when(leads[i])
            def _(i=i):
                for copy in moves(i, given[i]):
                    copy.wait()

        for copy in copies:
            copy.wait()

    base = 3 + picks - 1 + count + slots
    return pl.pallas_call(
        kernel,
        in_specs=[SMEM] * (3 + picks - 1)
        + [VMEM] * count
        + [VMEM] * slots
        + [HBM] * len(buffers),
        out_specs=[HBM] * 4,
        out_shape=shapes,
        scratch_shapes=[
            pltpu.VMEM((slots, 2, block, HEAD_DIM), jnp.bfloat16),
            pltpu.SemaphoreType.DMA((count * 2,)),
            pltpu.SemaphoreType.DMA((slots * 2,)),
        ],
        input_output_aliases={base + i: fresh + i for i in range(len(buffers))},
        compiler_params=pltpu.CompilerParams(vmem_limit_bytes=VMEM_LIMIT),
        name="finish",
    )(ids, chosen, span_pos, *wanted, *outs, *contributions, *buffers)


def per_device(query, keys, values, out_grad, span_pos, selected):
    count = lax.axis_size("head")
    seq_index = lax.axis_index("seq").astype(jnp.int32).reshape(1)
    me = lax.axis_index("head").astype(jnp.int32).reshape(1)
    ids = jnp.concatenate([seq_index, me])
    rows, width = query.shape
    block_rows = rows * count
    heads = keys.shape[1] // HEAD_DIM
    picks = selected.shape[1]
    distances = range(1, picks)

    wanted = [shifted(selected, "seq", -d) for d in distances]
    pieces = split_queries(query, out_grad, me, heads)
    moved = [[p[0]] + [flipped(p[r], "head", r) for r in range(1, count)] for p in pieces]
    outgoing = gather_blocks(keys, values, wanted, seq_index, block_rows, heads)
    arrived = [
        [shifted(outgoing[head][d - 1], "seq", d) for d in distances] for head in range(heads)
    ]
    buffers = []
    shapes = [jax.ShapeDtypeStruct(query.shape, query.dtype)] * 2
    shapes += [jax.ShapeDtypeStruct(keys.shape, keys.dtype)] * 2
    results = []
    for head in range(heads):
        outs, grads, cleared = attend(
            me, selected, span_pos, moved[head], keys, values, arrived[head], head
        )
        buffers += cleared
        returned = [shifted(grads[d], "seq", -d) for d in distances]
        outs = [outs[0]] + [flipped(outs[r], "head", r) for r in range(1, count)]
        results.append((outs, [grads[0]] + returned + [grads[picks]]))
    for head in range(heads):
        outs, contributions = results[head]
        buffers = finish(
            ids, selected, span_pos, wanted, outs, contributions, buffers, shapes, head, heads
        )
    return tuple(buffers)


def solution(mesh):
    in_specs = (
        P(("seq", "head"), None),
        P("seq", "head"),
        P("seq", "head"),
        P(("seq", "head"), None),
        P("seq"),
        P("seq", None),
    )
    out_specs = (
        P(("seq", "head"), None),
        P(("seq", "head"), None),
        P("seq", "head"),
        P("seq", "head"),
    )
    return jax.shard_map(
        per_device, mesh=mesh, in_specs=in_specs, out_specs=out_specs, check_vma=False
    )
```

```python
import functools
import math

import jax
import jax.numpy as jnp
from jax import lax
from jax.experimental import pallas as pl
from jax.experimental.pallas import tpu as pltpu
from jax.sharding import PartitionSpec as P

HEAD_DIM = 128
MASKED = -1e30
VMEM_LIMIT = 63 << 20

ROWS_ROWS = (((1,), (1,)), ((), ()))
ROWS_COLS = (((1,), (0,)), ((), ()))
HBM = pl.BlockSpec(memory_space=pl.ANY)
SMEM = pl.BlockSpec(memory_space=pltpu.SMEM)
VMEM = pl.BlockSpec(memory_space=pltpu.VMEM)


def shifted(value, axis, steps):
    count = lax.axis_size(axis)
    first, last = (max(0, -steps), min(count, count - steps))
    return lax.ppermute(value, axis, [(source, source + steps) for source in range(first, last)])


def exchanged(value, axis):
    return lax.all_to_all(value, axis, split_axis=0, concat_axis=0, tiled=True)


def dot(left, right, dims):
    return lax.dot_general(left, right, dims, preferred_element_type=jnp.float32)


def prepare(query, out_grad, keys, values, wanted, seq_index, heads):
    rows, width = query.shape
    devices = lax.axis_size("head")
    part = width // (devices * heads)
    block = rows * devices
    shard_blocks = keys.shape[0] // block
    count = len(wanted)
    pairs = heads * count

    def kernel(seq_ref, *refs):
        entries = refs[:count]
        q_ref, g_ref, k_ref, v_ref, queries_ref = refs[count : count + 5]
        outs = refs[count + 5 : count + 5 + pairs]
        held, held_queries, in_sem, out_sem = refs[count + 5 + pairs :]
        reads, writes = [], []

        def through(source, middle, target):
            slot = len(reads)
            reads.append(pltpu.make_async_copy(source, middle, in_sem.at[slot]))
            writes.append(pltpu.make_async_copy(middle, target, out_sem.at[slot]))

        for head in range(heads):
            for d in range(count):
                local = entries[d][0, d + 1] - seq_ref[0] * shard_blocks
                local = jnp.clip(local, 0, shard_blocks - 1)
                place = pl.ds(pl.multiple_of(local * block, block), block)
                cols = pl.ds(head * HEAD_DIM, HEAD_DIM)
                pair = head * count + d
                for which, source in enumerate((k_ref, v_ref)):
                    through(source.at[place, cols], held.at[pair, which], outs[pair].at[which])
        for device in range(devices):
            for head in range(heads):
                cols = pl.ds((device * heads + head) * part, part)
                for which, source in enumerate((q_ref, g_ref)):
                    row = head * 2 + which
                    through(
                        source.at[:, cols],
                        held_queries.at[device, row],
                        queries_ref.at[device, row],
                    )
        for read in reads:
            read.start()
        for read, write in zip(reads, writes):
            read.wait()
            write.start()
        for write in writes:
            write.wait()

    copies = pairs * 2 + devices * heads * 2
    flat = pl.pallas_call(
        kernel,
        in_specs=[SMEM] * (1 + count) + [HBM] * 4,
        out_specs=[HBM] * (1 + pairs),
        out_shape=[jax.ShapeDtypeStruct((devices, heads * 2, rows, part), query.dtype)]
        + [jax.ShapeDtypeStruct((2, block, HEAD_DIM), keys.dtype)] * pairs,
        scratch_shapes=[
            pltpu.VMEM((pairs, 2, block, HEAD_DIM), keys.dtype),
            pltpu.VMEM((devices, heads * 2, rows, part), query.dtype),
            pltpu.SemaphoreType.DMA((copies,)),
            pltpu.SemaphoreType.DMA((copies,)),
        ],
        compiler_params=pltpu.CompilerParams(vmem_limit_bytes=VMEM_LIMIT),
        name="prepare",
    )(seq_index, *wanted, query, out_grad, keys, values)
    return flat[0], [flat[1 + head * count : 1 + (head + 1) * count] for head in range(heads)]


def attend(chosen, span_pos, queries, keys, values, arrived, outs, head):
    count, _, rows, part = queries.shape
    group = part // HEAD_DIM
    block = count * rows
    picks = chosen.shape[1]
    slots = picks + 1
    shard_blocks = keys.shape[0] // block
    scale = HEAD_DIM**-0.5
    log2e = math.log2(math.e)
    fresh = 2 if head == 0 else 0
    clear_rows = math.gcd(keys.shape[0], 2048)
    clear_steps = keys.shape[0] // clear_rows
    clear_scratch = []
    if fresh:
        clear_scratch.append(pltpu.VMEM((clear_rows, keys.shape[1]), keys.dtype))
        clear_scratch.append(pltpu.SemaphoreType.DMA((fresh * clear_steps,)))

    def kernel(chosen_ref, pos_ref, queries_ref, *refs):
        first_k, first_v, own_k, own_v = refs[:4]
        refs = refs[4:]
        arrived_refs, refs = refs[: picks - 1], refs[picks - 1 + len(outs) :]
        out_ref, refs = refs[0], refs[1:]
        grad_refs, refs = refs[:slots], refs[slots:]
        zero_refs, refs = refs[:fresh], refs[fresh:]
        s_ref, acc_k, acc_v, k_t, v_t = refs[:5]
        key_refs = [first_k] + [ref.at[0] for ref in arrived_refs] + [own_k]
        value_refs = [first_v] + [ref.at[1] for ref in arrived_refs] + [own_v]
        spans = [slice(slot * block, (slot + 1) * block) for slot in range(slots)]
        step = pl.program_id(0)
        clears = []
        if fresh:
            blank, blank_sem = refs[5:]
            for which, target in enumerate(zero_refs):
                for part in range(clear_steps):
                    place = target.at[pl.ds(part * clear_rows, clear_rows)]
                    slot = blank_sem.at[which * clear_steps + part]
                    clears.append(pltpu.make_async_copy(blank, place, slot))

        @pl.when(step == 0)
        def _():
            if fresh:
                blank[...] = jnp.zeros_like(blank)
            for clear in clears:
                clear.start()
            for slot in range(slots):
                k_t[:, spans[slot]] = key_refs[slot][...].T
                v_t[:, spans[slot]] = value_refs[slot][...].T

        q = queries_ref[:, 0].reshape(block, HEAD_DIM)
        g = queries_ref[:, 1].reshape(block, HEAD_DIM)
        top = jnp.full((1, block), MASKED, jnp.float32)
        for slot in range(slots):
            s = dot(key_refs[slot][...], q, ROWS_ROWS) * (scale * log2e)
            if slot == picks:
                key_pos = lax.broadcasted_iota(jnp.int32, (block, block), 0)
                query_pos = lax.broadcasted_iota(jnp.int32, (block, block), 1)
                s = jnp.where(key_pos <= query_pos, s, MASKED)
            else:
                s = jnp.where(chosen_ref[0, slot] >= 0, s, MASKED)
            s_ref[spans[slot]] = s
            top = jnp.maximum(top, jnp.max(s, axis=0, keepdims=True))
        total = jnp.zeros((1, block), jnp.float32)
        for slot in range(slots):
            e = jnp.exp2(s_ref[spans[slot]] - top)
            s_ref[spans[slot]] = e
            total = total + jnp.sum(e, axis=0, keepdims=True)
        inverse = 1.0 / total
        o_t = jnp.zeros((HEAD_DIM, block), jnp.float32)
        for slot in range(slots):
            w = s_ref[spans[slot]] * inverse
            s_ref[spans[slot]] = w
            low = w.astype(jnp.bfloat16)
            o_t = o_t + dot(v_t[:, spans[slot]], low, ROWS_COLS)
            before = jnp.where(step == 0, 0.0, acc_v[spans[slot]])
            acc_v[spans[slot]] = before + dot(low, g, ROWS_COLS)
        o_t = o_t.astype(jnp.bfloat16).astype(jnp.float32)
        delta = jnp.sum(g.T.astype(jnp.float32) * o_t, axis=0, keepdims=True)
        q_t = jnp.zeros((HEAD_DIM, block), jnp.float32)
        for slot in range(slots):
            w_grad = dot(value_refs[slot][...], g, ROWS_ROWS)
            s_grad = (s_ref[spans[slot]] * (w_grad - delta)).astype(jnp.bfloat16)
            q_t = q_t + dot(k_t[:, spans[slot]], s_grad, ROWS_COLS)
            before = jnp.where(step == 0, 0.0, acc_k[spans[slot]])
            acc_k[spans[slot]] = before + dot(s_grad, q, ROWS_COLS)
        o = o_t.T.astype(jnp.bfloat16)
        q_grad = (q_t * scale).T.astype(jnp.bfloat16)
        out_ref[:, 0] = o.reshape(count, rows, HEAD_DIM)
        out_ref[:, 1] = q_grad.reshape(count, rows, HEAD_DIM)

        @pl.when(step == group - 1)
        def _():
            for slot in range(slots):
                grad_refs[slot][0] = (acc_k[spans[slot]] * scale).astype(jnp.bfloat16)
                grad_refs[slot][1] = acc_v[spans[slot]].astype(jnp.bfloat16)
            for clear in clears:
                clear.wait()

    def first_index(step, chosen, pos):
        return (jnp.maximum(lax.rem(chosen[0, 0], shard_blocks), 0), head)

    def own_index(step, chosen, pos):
        return (pos[0], head)

    def whole_index(step, chosen, pos):
        return (0, 0, 0)

    piece = pl.BlockSpec((count, 2, rows, HEAD_DIM), lambda step, chosen, pos: (0, head, 0, step))
    pair = pl.BlockSpec((2, block, HEAD_DIM), whole_index)
    flops = 12 * block * slots * block * HEAD_DIM * group
    result = pl.pallas_call(
        kernel,
        grid_spec=pltpu.PrefetchScalarGridSpec(
            num_scalar_prefetch=2,
            grid=(group,),
            in_specs=[piece]
            + [pl.BlockSpec((block, HEAD_DIM), first_index)] * 2
            + [pl.BlockSpec((block, HEAD_DIM), own_index)] * 2
            + [pair] * (picks - 1)
            + [HBM] * len(outs),
            out_specs=[piece] + [pair] * slots + [HBM] * fresh,
            scratch_shapes=[
                pltpu.VMEM((slots * block, block), jnp.float32),
                pltpu.VMEM((slots * block, HEAD_DIM), jnp.float32),
                pltpu.VMEM((slots * block, HEAD_DIM), jnp.float32),
                pltpu.VMEM((HEAD_DIM, slots * block), jnp.bfloat16),
                pltpu.VMEM((HEAD_DIM, slots * block), jnp.bfloat16),
            ]
            + clear_scratch,
        ),
        out_shape=[jax.ShapeDtypeStruct(queries.shape, jnp.bfloat16)]
        + [jax.ShapeDtypeStruct((2, block, HEAD_DIM), jnp.bfloat16)] * slots
        + [jax.ShapeDtypeStruct(keys.shape, keys.dtype)] * fresh,
        compiler_params=pltpu.CompilerParams(vmem_limit_bytes=VMEM_LIMIT),
        cost_estimate=pl.CostEstimate(
            flops=flops, bytes_accessed=8 << 20, transcendentals=block * block * slots * group
        ),
        input_output_aliases={2 + 5 + picks - 1 + i: i for i in range(len(outs))},
        name="attend",
    )(chosen, span_pos, queries, keys, values, keys, values, *arrived, *outs)
    return (result[0], result[1 : 1 + slots], result[1 + slots :])


def finish(seq_index, chosen, span_pos, wanted, outs, contributions, buffers, shapes, head):
    slots = len(contributions)
    picks = slots - 1
    block = contributions[0].shape[1]
    shapes = shapes if outs else shapes[2:]

    def kernel(seq_ref, chosen_ref, pos_ref, *refs):
        wanted_refs, refs = refs[: picks - 1], refs[picks - 1 :]
        out_refs, refs = refs[: len(outs)], refs[len(outs) :]
        given, refs = refs[:slots], refs[slots:]
        refs = refs[len(buffers) :]
        row_refs, refs = refs[: len(shapes) - 2], refs[len(shapes) - 2 :]
        key_ref, value_ref, held, held_rows, sums, read_sem, row_sem, out_sem, grad_sem = refs
        seq = seq_ref[0]
        shard_blocks = key_ref.shape[0] // block
        copies, row_reads = [], []
        for out_ref in out_refs:
            devices, rows, _, part = out_ref.shape
            row_reads.append(pltpu.make_async_copy(out_ref, held_rows, row_sem))
            for place in range(devices * rows // 2):
                device, head_of = place // (rows // 2), place % (rows // 2)
                for which, target in enumerate(row_refs):
                    slot = place * 2 + which
                    piece = (device, head_of * 2 + which)
                    columns = target.at[:, pl.ds(place * part, part)]
                    middle = held_rows.at[piece]
                    copies.append(pltpu.make_async_copy(middle, columns, out_sem.at[slot]))
        reads = [
            pltpu.make_async_copy(given[i], held.at[i], read_sem.at[i]) for i in range(slots)
        ]
        for read in reads + row_reads:
            read.start()
        targets = [jnp.where(chosen_ref[0, 0] >= 0, chosen_ref[0, 0] - seq * shard_blocks, -1)]
        for d in range(1, picks):
            above = seq + d < lax.axis_size("seq")
            local = wanted_refs[d - 1][0, d] - seq * shard_blocks
            targets.append(jnp.where(above, local, -1))
        targets.append(pos_ref[0])
        present = [(t >= 0) & (t < shard_blocks) for t in targets]
        same = {}
        for i in range(slots):
            for j in range(i + 1, slots):
                same[i, j] = present[i] & (targets[i] == targets[j])

        def moves(i, source):
            start = pl.multiple_of(jnp.clip(targets[i], 0, shard_blocks - 1) * block, block)
            place = (pl.ds(start, block), pl.ds(head * HEAD_DIM, HEAD_DIM))
            return [
                pltpu.make_async_copy(source.at[which], target.at[place], grad_sem.at[i * 2 + which])
                for which, target in enumerate((key_ref, value_ref))
            ]

        leads = []
        for read in reads:
            read.wait()
        for i in range(slots):
            lead = present[i]
            for j in range(i):
                lead = lead & jnp.logical_not(same[j, i])
            shared = jnp.bool_(False)
            for j in range(i + 1, slots):
                shared = shared | same[i, j]
            leads.append(lead)

            @pl.when(lead & jnp.logical_not(shared))
            def _(i=i):
                for copy in moves(i, held.at[i]):
                    copy.start()

            @pl.when(lead & shared)
            def _(i=i):
                value = held[i].astype(jnp.float32)
                for j in range(i + 1, slots):
                    value = value + jnp.where(same[i, j], held[j].astype(jnp.float32), 0.0)
                sums[i] = value.astype(jnp.bfloat16)
                for copy in moves(i, sums.at[i]):
                    copy.start()

        for read in row_reads:
            read.wait()
        for copy in copies:
            copy.start()
        for i in range(slots):

            @pl.when(leads[i])
            def _(i=i):
                for copy in moves(i, held.at[i]):
                    copy.wait()

        for copy in copies:
            copy.wait()

    out_copies = outs[0].shape[0] * outs[0].shape[1] if outs else 1
    base = 3 + picks - 1 + len(outs) + slots
    return pl.pallas_call(
        kernel,
        in_specs=[SMEM] * (3 + picks - 1)
        + [HBM] * (len(outs) + slots + len(buffers)),
        out_specs=[HBM] * len(shapes),
        out_shape=shapes,
        scratch_shapes=[
            pltpu.VMEM((slots, 2, block, HEAD_DIM), jnp.bfloat16),
            pltpu.VMEM(outs[0].shape if outs else (16, HEAD_DIM), jnp.bfloat16),
            pltpu.VMEM((slots, 2, block, HEAD_DIM), jnp.bfloat16),
            pltpu.SemaphoreType.DMA((slots,)),
            pltpu.SemaphoreType.DMA,
            pltpu.SemaphoreType.DMA((out_copies,)),
            pltpu.SemaphoreType.DMA((slots * 2,)),
        ],
        input_output_aliases={base + i: len(shapes) - 2 + i for i in range(2)},
        compiler_params=pltpu.CompilerParams(vmem_limit_bytes=VMEM_LIMIT),
        name="finish",
    )(seq_index, chosen, span_pos, *wanted, *outs, *contributions, *buffers)


def per_device(query, keys, values, out_grad, span_pos, selected):
    seq_index = lax.axis_index("seq").astype(jnp.int32).reshape(1)
    heads = keys.shape[1] // HEAD_DIM
    distances = range(1, selected.shape[1])

    wanted = [shifted(selected, "seq", -d) for d in distances]
    queries, outgoing = prepare(query, out_grad, keys, values, wanted, seq_index, heads)
    queries = exchanged(queries, "head")
    arrived = [[shifted(piece[d - 1], "seq", d) for d in distances] for piece in outgoing]
    shapes = [jax.ShapeDtypeStruct(query.shape, query.dtype)] * 2
    shapes += [jax.ShapeDtypeStruct(keys.shape, keys.dtype)] * 2
    buffers, outs, results = [], [], []
    for head in range(heads):
        out, grads, cleared = attend(
            selected, span_pos, queries, keys, values, arrived[head], outs, head
        )
        buffers += cleared
        if results:
            out, grads, results[-1] = lax.optimization_barrier((out, grads, results[-1]))
        outs = [out]
        returned = [shifted(grads[d], "seq", -d) for d in distances]
        results.append([grads[0]] + returned + [grads[-1]])
    out = exchanged(outs[0], "head")
    for head in range(heads):
        given = [out] if head == heads - 1 else []
        buffers = finish(
            seq_index, selected, span_pos, wanted, given, results[head], buffers, shapes, head
        )
    return tuple(buffers)


def solution(mesh):
    in_specs = (
        P(("seq", "head"), None),
        P("seq", "head"),
        P("seq", "head"),
        P(("seq", "head"), None),
        P("seq"),
        P("seq", None),
    )
    out_specs = (
        P(("seq", "head"), None),
        P(("seq", "head"), None),
        P("seq", "head"),
        P("seq", "head"),
    )
    return jax.shard_map(
        per_device, mesh=mesh, in_specs=in_specs, out_specs=out_specs, check_vma=False
    )
```

```python
import functools
import math

import jax
import jax.numpy as jnp
from jax import lax
from jax.experimental import pallas as pl
from jax.experimental.pallas import tpu as pltpu
from jax.sharding import PartitionSpec as P

HEAD_DIM = 128
MASKED = -1e30
VMEM_LIMIT = 63 << 20

ROWS_ROWS = (((1,), (1,)), ((), ()))
ROWS_COLS = (((1,), (0,)), ((), ()))
HBM = pl.BlockSpec(memory_space=pl.ANY)
SMEM = pl.BlockSpec(memory_space=pltpu.SMEM)
VMEM = pl.BlockSpec(memory_space=pltpu.VMEM)


def shifted(value, axis, steps):
    count = lax.axis_size(axis)
    first, last = (max(0, -steps), min(count, count - steps))
    return lax.ppermute(value, axis, [(source, source + steps) for source in range(first, last)])


def exchanged(value, axis):
    return lax.all_to_all(value, axis, split_axis=0, concat_axis=0, tiled=True)


def dot(left, right, dims):
    return lax.dot_general(left, right, dims, preferred_element_type=jnp.float32)


def prepare(query, out_grad, keys, values, wanted, seq_index, heads):
    rows, width = query.shape
    devices = lax.axis_size("head")
    part = width // (devices * heads)
    block = rows * devices
    shard_blocks = keys.shape[0] // block
    count = len(wanted)
    pairs = heads * count

    def kernel(seq_ref, *refs):
        entries = refs[:count]
        q_ref, g_ref, k_ref, v_ref, queries_ref = refs[count : count + 5]
        outs = refs[count + 5 : count + 5 + pairs]
        held, held_queries, in_sem, out_sem = refs[count + 5 + pairs :]
        reads, writes = [], []

        def through(source, middle, target):
            slot = len(reads)
            reads.append(pltpu.make_async_copy(source, middle, in_sem.at[slot]))
            writes.append(pltpu.make_async_copy(middle, target, out_sem.at[slot]))

        for head in range(heads):
            for d in range(count):
                local = entries[d][0, d + 1] - seq_ref[0] * shard_blocks
                local = jnp.clip(local, 0, shard_blocks - 1)
                place = pl.ds(pl.multiple_of(local * block, block), block)
                cols = pl.ds(head * HEAD_DIM, HEAD_DIM)
                pair = head * count + d
                for which, source in enumerate((k_ref, v_ref)):
                    through(source.at[place, cols], held.at[pair, which], outs[pair].at[which])
        for device in range(devices):
            for head in range(heads):
                cols = pl.ds((device * heads + head) * part, part)
                for which, source in enumerate((q_ref, g_ref)):
                    row = head * 2 + which
                    through(
                        source.at[:, cols],
                        held_queries.at[device, row],
                        queries_ref.at[device, row],
                    )
        for read in reads:
            read.start()
        for read, write in zip(reads, writes):
            read.wait()
            write.start()
        for write in writes:
            write.wait()

    copies = pairs * 2 + devices * heads * 2
    flat = pl.pallas_call(
        kernel,
        in_specs=[SMEM] * (1 + count) + [HBM] * 4,
        out_specs=[HBM] * (1 + pairs),
        out_shape=[jax.ShapeDtypeStruct((devices, heads * 2, rows, part), query.dtype)]
        + [jax.ShapeDtypeStruct((2, block, HEAD_DIM), keys.dtype)] * pairs,
        scratch_shapes=[
            pltpu.VMEM((pairs, 2, block, HEAD_DIM), keys.dtype),
            pltpu.VMEM((devices, heads * 2, rows, part), query.dtype),
            pltpu.SemaphoreType.DMA((copies,)),
            pltpu.SemaphoreType.DMA((copies,)),
        ],
        compiler_params=pltpu.CompilerParams(vmem_limit_bytes=VMEM_LIMIT),
        name="prepare",
    )(seq_index, *wanted, query, out_grad, keys, values)
    return flat[0], [flat[1 + head * count : 1 + (head + 1) * count] for head in range(heads)]


def attend(chosen, span_pos, queries, keys, values, arrived, outs, head):
    count, _, rows, part = queries.shape
    group = part // HEAD_DIM
    block = count * rows
    picks = chosen.shape[1]
    slots = picks + 1
    shard_blocks = keys.shape[0] // block
    scale = HEAD_DIM**-0.5
    log2e = math.log2(math.e)
    parts = [range((slots + 1) // 2), range((slots + 1) // 2, slots)]
    fresh = 2 if head == 0 else 0
    clear_rows = math.gcd(keys.shape[0], 2048)
    clear_steps = keys.shape[0] // clear_rows
    clear_scratch = []
    if fresh:
        clear_scratch.append(pltpu.VMEM((clear_rows, keys.shape[1]), keys.dtype))
        clear_scratch.append(pltpu.SemaphoreType.DMA((fresh * clear_steps,)))

    def kernel(chosen_ref, pos_ref, queries_ref, *refs):
        first_k, first_v, own_k, own_v = refs[:4]
        refs = refs[4:]
        arrived_refs, refs = refs[: picks - 1], refs[picks - 1 + len(outs) :]
        out_ref, refs = refs[0], refs[1:]
        grad_refs, refs = refs[:slots], refs[slots:]
        zero_refs, refs = refs[:fresh], refs[fresh:]
        s_ref, acc_k, acc_v, k_t, v_t, k_all, v_all = refs[:7]
        key_refs = [first_k] + [ref.at[0] for ref in arrived_refs] + [own_k]
        value_refs = [first_v] + [ref.at[1] for ref in arrived_refs] + [own_v]
        spans = [slice(slot * block, (slot + 1) * block) for slot in range(slots)]
        step = pl.program_id(0)
        clears = []
        if fresh:
            blank, blank_sem = refs[7:]
            for which, target in enumerate(zero_refs):
                for part in range(clear_steps):
                    place = target.at[pl.ds(part * clear_rows, clear_rows)]
                    slot = blank_sem.at[which * clear_steps + part]
                    clears.append(pltpu.make_async_copy(blank, place, slot))

        @pl.when(step == 0)
        def _():
            if fresh:
                blank[...] = jnp.zeros_like(blank)
            for clear in clears:
                clear.start()
            acc_k[...] = jnp.zeros_like(acc_k)
            acc_v[...] = jnp.zeros_like(acc_v)
            for slot in range(slots):
                k_all[spans[slot]] = key_refs[slot][...]
                v_all[spans[slot]] = value_refs[slot][...]
                k_t[:, spans[slot]] = key_refs[slot][...].T
                v_t[:, spans[slot]] = value_refs[slot][...].T

        q = queries_ref[:, 0].reshape(block, HEAD_DIM)
        g = queries_ref[:, 1].reshape(block, HEAD_DIM)
        top = jnp.full((1, block), MASKED, jnp.float32)
        for part_slots in parts:
            start = part_slots[0] * block
            rows_of = slice(start, (part_slots[-1] + 1) * block)
            scores = dot(k_all[rows_of], q, ROWS_ROWS) * (scale * log2e)
            for slot in part_slots:
                s = scores[slot * block - start : (slot + 1) * block - start]
                if slot == picks:
                    key_pos = lax.broadcasted_iota(jnp.int32, (block, block), 0)
                    query_pos = lax.broadcasted_iota(jnp.int32, (block, block), 1)
                    s = jnp.where(key_pos <= query_pos, s, MASKED)
                s_ref[spans[slot]] = s
                slot_top = jnp.max(s, axis=0, keepdims=True)
                if slot < picks:
                    slot_top = jnp.where(chosen_ref[0, slot] >= 0, slot_top, MASKED)
                top = jnp.maximum(top, slot_top)
        total = jnp.zeros((1, block), jnp.float32)
        for slot in range(slots):
            level = top if slot == picks else jnp.where(chosen_ref[0, slot] >= 0, top, -MASKED)
            e = jnp.exp2(s_ref[spans[slot]] - level)
            s_ref[spans[slot]] = e
            total = total + jnp.sum(e, axis=0, keepdims=True)
        inverse = 1.0 / total
        o_t = jnp.zeros((HEAD_DIM, block), jnp.float32)
        for part_slots in parts:
            rows_of = slice(part_slots[0] * block, (part_slots[-1] + 1) * block)
            w = s_ref[rows_of] * inverse
            s_ref[rows_of] = w
            low = w.astype(jnp.bfloat16)
            o_t = o_t + dot(v_t[:, rows_of], low, ROWS_COLS)
            acc_v[rows_of] += dot(low, g, ROWS_COLS)
        o_t = o_t.astype(jnp.bfloat16).astype(jnp.float32)
        delta = jnp.sum(g.T.astype(jnp.float32) * o_t, axis=0, keepdims=True)
        q_t = jnp.zeros((HEAD_DIM, block), jnp.float32)
        for part_slots in parts:
            rows_of = slice(part_slots[0] * block, (part_slots[-1] + 1) * block)
            w_grad = dot(v_all[rows_of], g, ROWS_ROWS)
            s_grad = (s_ref[rows_of] * (w_grad - delta)).astype(jnp.bfloat16)
            q_t = q_t + dot(k_t[:, rows_of], s_grad, ROWS_COLS)
            acc_k[rows_of] += dot(s_grad, q, ROWS_COLS)
        o = o_t.T.astype(jnp.bfloat16)
        q_grad = (q_t * scale).T.astype(jnp.bfloat16)
        out_ref[:, 0] = o.reshape(count, rows, HEAD_DIM)
        out_ref[:, 1] = q_grad.reshape(count, rows, HEAD_DIM)

        @pl.when(step == group - 1)
        def _():
            for slot in range(slots):
                grad_refs[slot][0] = (acc_k[spans[slot]] * scale).astype(jnp.bfloat16)
                grad_refs[slot][1] = acc_v[spans[slot]].astype(jnp.bfloat16)
            for clear in clears:
                clear.wait()

    def first_index(step, chosen, pos):
        return (jnp.maximum(lax.rem(chosen[0, 0], shard_blocks), 0), head)

    def own_index(step, chosen, pos):
        return (pos[0], head)

    def whole_index(step, chosen, pos):
        return (0, 0, 0)

    piece = pl.BlockSpec((count, 2, rows, HEAD_DIM), lambda step, chosen, pos: (0, head, 0, step))
    pair = pl.BlockSpec((2, block, HEAD_DIM), whole_index)
    flops = 12 * block * slots * block * HEAD_DIM * group
    result = pl.pallas_call(
        kernel,
        grid_spec=pltpu.PrefetchScalarGridSpec(
            num_scalar_prefetch=2,
            grid=(group,),
            in_specs=[piece]
            + [pl.BlockSpec((block, HEAD_DIM), first_index)] * 2
            + [pl.BlockSpec((block, HEAD_DIM), own_index)] * 2
            + [pair] * (picks - 1)
            + [HBM] * len(outs),
            out_specs=[piece] + [pair] * slots + [HBM] * fresh,
            scratch_shapes=[
                pltpu.VMEM((slots * block, block), jnp.float32),
                pltpu.VMEM((slots * block, HEAD_DIM), jnp.float32),
                pltpu.VMEM((slots * block, HEAD_DIM), jnp.float32),
                pltpu.VMEM((HEAD_DIM, slots * block), jnp.bfloat16),
                pltpu.VMEM((HEAD_DIM, slots * block), jnp.bfloat16),
                pltpu.VMEM((slots * block, HEAD_DIM), jnp.bfloat16),
                pltpu.VMEM((slots * block, HEAD_DIM), jnp.bfloat16),
            ]
            + clear_scratch,
        ),
        out_shape=[jax.ShapeDtypeStruct(queries.shape, jnp.bfloat16)]
        + [jax.ShapeDtypeStruct((2, block, HEAD_DIM), jnp.bfloat16)] * slots
        + [jax.ShapeDtypeStruct(keys.shape, keys.dtype)] * fresh,
        compiler_params=pltpu.CompilerParams(vmem_limit_bytes=VMEM_LIMIT),
        cost_estimate=pl.CostEstimate(
            flops=flops, bytes_accessed=8 << 20, transcendentals=block * block * slots * group
        ),
        input_output_aliases={2 + 5 + picks - 1 + i: i for i in range(len(outs))},
        name="attend",
    )(chosen, span_pos, queries, keys, values, keys, values, *arrived, *outs)
    return (result[0], result[1 : 1 + slots], result[1 + slots :])


def finish(seq_index, chosen, span_pos, wanted, outs, contributions, buffers, shapes, head):
    slots = len(contributions)
    picks = slots - 1
    block = contributions[0].shape[1]
    shapes = shapes if outs else shapes[2:]

    def kernel(seq_ref, chosen_ref, pos_ref, *refs):
        wanted_refs, refs = refs[: picks - 1], refs[picks - 1 :]
        out_refs, refs = refs[: len(outs)], refs[len(outs) :]
        given, refs = refs[:slots], refs[slots:]
        refs = refs[len(buffers) :]
        row_refs, refs = refs[: len(shapes) - 2], refs[len(shapes) - 2 :]
        key_ref, value_ref, held, held_rows, sums, read_sem, row_sem, out_sem, grad_sem = refs
        seq = seq_ref[0]
        shard_blocks = key_ref.shape[0] // block
        copies, row_reads = [], []
        for out_ref in out_refs:
            devices, rows, _, part = out_ref.shape
            row_reads.append(pltpu.make_async_copy(out_ref, held_rows, row_sem))
            for place in range(devices * rows // 2):
                device, head_of = place // (rows // 2), place % (rows // 2)
                for which, target in enumerate(row_refs):
                    slot = place * 2 + which
                    piece = (device, head_of * 2 + which)
                    columns = target.at[:, pl.ds(place * part, part)]
                    middle = held_rows.at[piece]
                    copies.append(pltpu.make_async_copy(middle, columns, out_sem.at[slot]))
        reads = [
            pltpu.make_async_copy(given[i], held.at[i], read_sem.at[i]) for i in range(slots)
        ]
        for read in reads + row_reads:
            read.start()
        targets = [jnp.where(chosen_ref[0, 0] >= 0, chosen_ref[0, 0] - seq * shard_blocks, -1)]
        for d in range(1, picks):
            above = seq + d < lax.axis_size("seq")
            local = wanted_refs[d - 1][0, d] - seq * shard_blocks
            targets.append(jnp.where(above, local, -1))
        targets.append(pos_ref[0])
        present = [(t >= 0) & (t < shard_blocks) for t in targets]
        same = {}
        for i in range(slots):
            for j in range(i + 1, slots):
                same[i, j] = present[i] & (targets[i] == targets[j])

        def moves(i, source):
            start = pl.multiple_of(jnp.clip(targets[i], 0, shard_blocks - 1) * block, block)
            place = (pl.ds(start, block), pl.ds(head * HEAD_DIM, HEAD_DIM))
            return [
                pltpu.make_async_copy(source.at[which], target.at[place], grad_sem.at[i * 2 + which])
                for which, target in enumerate((key_ref, value_ref))
            ]

        leads = []
        for read in reads:
            read.wait()
        for i in range(slots):
            lead = present[i]
            for j in range(i):
                lead = lead & jnp.logical_not(same[j, i])
            shared = jnp.bool_(False)
            for j in range(i + 1, slots):
                shared = shared | same[i, j]
            leads.append(lead)

            @pl.when(lead & jnp.logical_not(shared))
            def _(i=i):
                for copy in moves(i, held.at[i]):
                    copy.start()

            @pl.when(lead & shared)
            def _(i=i):
                value = held[i].astype(jnp.float32)
                for j in range(i + 1, slots):
                    value = value + jnp.where(same[i, j], held[j].astype(jnp.float32), 0.0)
                sums[i] = value.astype(jnp.bfloat16)
                for copy in moves(i, sums.at[i]):
                    copy.start()

        for read in row_reads:
            read.wait()
        for copy in copies:
            copy.start()
        for i in range(slots):

            @pl.when(leads[i])
            def _(i=i):
                for copy in moves(i, held.at[i]):
                    copy.wait()

        for copy in copies:
            copy.wait()

    out_copies = outs[0].shape[0] * outs[0].shape[1] if outs else 1
    base = 3 + picks - 1 + len(outs) + slots
    return pl.pallas_call(
        kernel,
        in_specs=[SMEM] * (3 + picks - 1)
        + [HBM] * (len(outs) + slots + len(buffers)),
        out_specs=[HBM] * len(shapes),
        out_shape=shapes,
        scratch_shapes=[
            pltpu.VMEM((slots, 2, block, HEAD_DIM), jnp.bfloat16),
            pltpu.VMEM(outs[0].shape if outs else (16, HEAD_DIM), jnp.bfloat16),
            pltpu.VMEM((slots, 2, block, HEAD_DIM), jnp.bfloat16),
            pltpu.SemaphoreType.DMA((slots,)),
            pltpu.SemaphoreType.DMA,
            pltpu.SemaphoreType.DMA((out_copies,)),
            pltpu.SemaphoreType.DMA((slots * 2,)),
        ],
        input_output_aliases={base + i: len(shapes) - 2 + i for i in range(2)},
        compiler_params=pltpu.CompilerParams(vmem_limit_bytes=VMEM_LIMIT),
        name="finish",
    )(seq_index, chosen, span_pos, *wanted, *outs, *contributions, *buffers)


def per_device(query, keys, values, out_grad, span_pos, selected):
    seq_index = lax.axis_index("seq").astype(jnp.int32).reshape(1)
    heads = keys.shape[1] // HEAD_DIM
    distances = range(1, selected.shape[1])

    wanted = [shifted(selected, "seq", -d) for d in distances]
    queries, outgoing = prepare(query, out_grad, keys, values, wanted, seq_index, heads)
    queries = exchanged(queries, "head")
    arrived = [[shifted(piece[d - 1], "seq", d) for d in distances] for piece in outgoing]
    shapes = [jax.ShapeDtypeStruct(query.shape, query.dtype)] * 2
    shapes += [jax.ShapeDtypeStruct(keys.shape, keys.dtype)] * 2
    buffers, outs, results = [], [], []
    for head in range(heads):
        out, grads, cleared = attend(
            selected, span_pos, queries, keys, values, arrived[head], outs, head
        )
        buffers += cleared
        if results:
            out, grads, results[-1] = lax.optimization_barrier((out, grads, results[-1]))
        outs = [out]
        returned = [shifted(grads[d], "seq", -d) for d in distances]
        results.append([grads[0]] + returned + [grads[-1]])
    out = exchanged(outs[0], "head")
    for head in range(heads):
        given = [out] if head == heads - 1 else []
        buffers = finish(
            seq_index, selected, span_pos, wanted, given, results[head], buffers, shapes, head
        )
    return tuple(buffers)


def solution(mesh):
    in_specs = (
        P(("seq", "head"), None),
        P("seq", "head"),
        P("seq", "head"),
        P(("seq", "head"), None),
        P("seq"),
        P("seq", None),
    )
    out_specs = (
        P(("seq", "head"), None),
        P(("seq", "head"), None),
        P("seq", "head"),
        P("seq", "head"),
    )
    return jax.shard_map(
        per_device, mesh=mesh, in_specs=in_specs, out_specs=out_specs, check_vma=False
    )
```

```python
import functools
import math

import jax
import jax.numpy as jnp
from jax import lax
from jax.experimental import pallas as pl
from jax.experimental.pallas import tpu as pltpu
from jax.sharding import PartitionSpec as P

HEAD_DIM = 128
MASKED = -1e30
VMEM_LIMIT = 63 << 20

ROWS_ROWS = (((1,), (1,)), ((), ()))
ROWS_COLS = (((1,), (0,)), ((), ()))
HBM = pl.BlockSpec(memory_space=pl.ANY)
SMEM = pl.BlockSpec(memory_space=pltpu.SMEM)
VMEM = pl.BlockSpec(memory_space=pltpu.VMEM)


def shifted(value, axis, steps):
    count = lax.axis_size(axis)
    first, last = (max(0, -steps), min(count, count - steps))
    return lax.ppermute(value, axis, [(source, source + steps) for source in range(first, last)])


def exchanged(value, axis):
    return lax.all_to_all(value, axis, split_axis=0, concat_axis=0, tiled=True)


def dot(left, right, dims):
    return lax.dot_general(left, right, dims, preferred_element_type=jnp.float32)


def prepare(query, out_grad, keys, values, wanted, seq_index, heads):
    rows, width = query.shape
    devices = lax.axis_size("head")
    part = width // (devices * heads)
    block = rows * devices
    shard_blocks = keys.shape[0] // block
    count = len(wanted)
    pairs = heads * count

    def kernel(seq_ref, *refs):
        entries = refs[:count]
        q_ref, g_ref, k_ref, v_ref, queries_ref = refs[count : count + 5]
        outs = refs[count + 5 : count + 5 + pairs]
        held, held_queries, in_sem, out_sem = refs[count + 5 + pairs :]
        reads, writes = [], []

        def read(source, middle):
            reads.append(pltpu.make_async_copy(source, middle, in_sem.at[len(reads)]))
            writes.append([])

        def write(middle, target):
            slot = out_sem.at[sum(map(len, writes))]
            writes[-1].append(pltpu.make_async_copy(middle, target, slot))

        for d in range(count):
            local = entries[d][0, d + 1] - seq_ref[0] * shard_blocks
            local = jnp.clip(local, 0, shard_blocks - 1)
            place = pl.ds(pl.multiple_of(local * block, block), block)
            for which, source in enumerate((k_ref, v_ref)):
                read(source.at[place], held.at[d, which])
                for head in range(heads):
                    cols = pl.ds(head * HEAD_DIM, HEAD_DIM)
                    write(held.at[d, which, :, cols], outs[head * count + d].at[which])
        for which, source in enumerate((q_ref, g_ref)):
            read(source, held_queries.at[which])
            for device in range(devices):
                for head in range(heads):
                    cols = pl.ds((device * heads + head) * part, part)
                    write(
                        held_queries.at[which, :, cols], queries_ref.at[device, head * 2 + which]
                    )
        for copy in reads:
            copy.start()
        for copy, following in zip(reads, writes):
            copy.wait()
            for later in following:
                later.start()
        for following in writes:
            for later in following:
                later.wait()

    copies = pairs * 2 + devices * heads * 2
    flat = pl.pallas_call(
        kernel,
        in_specs=[SMEM] * (1 + count) + [HBM] * 4,
        out_specs=[HBM] * (1 + pairs),
        out_shape=[jax.ShapeDtypeStruct((devices, heads * 2, rows, part), query.dtype)]
        + [jax.ShapeDtypeStruct((2, block, HEAD_DIM), keys.dtype)] * pairs,
        scratch_shapes=[
            pltpu.VMEM((count, 2, block, heads * HEAD_DIM), keys.dtype),
            pltpu.VMEM((2, rows, width), query.dtype),
            pltpu.SemaphoreType.DMA((count * 2 + 2,)),
            pltpu.SemaphoreType.DMA((copies,)),
        ],
        compiler_params=pltpu.CompilerParams(vmem_limit_bytes=VMEM_LIMIT),
        name="prepare",
    )(seq_index, *wanted, query, out_grad, keys, values)
    return flat[0], [flat[1 + head * count : 1 + (head + 1) * count] for head in range(heads)]


def attend(chosen, span_pos, queries, keys, values, arrived, outs, head):
    count, _, rows, part = queries.shape
    group = part // HEAD_DIM
    block = count * rows
    picks = chosen.shape[1]
    slots = picks + 1
    shard_blocks = keys.shape[0] // block
    scale = HEAD_DIM**-0.5
    log2e = math.log2(math.e)
    parts = [range((slots + 1) // 2), range((slots + 1) // 2, slots)]
    fresh = 2 if head == 0 else 0
    clear_rows = math.gcd(keys.shape[0], 2048)
    clear_steps = keys.shape[0] // clear_rows
    clear_scratch = []
    if fresh:
        clear_scratch.append(pltpu.VMEM((clear_rows, keys.shape[1]), keys.dtype))
        clear_scratch.append(pltpu.SemaphoreType.DMA((fresh * clear_steps,)))

    def kernel(chosen_ref, pos_ref, queries_ref, *refs):
        first_k, first_v, own_k, own_v = refs[:4]
        refs = refs[4:]
        arrived_refs, refs = refs[: picks - 1], refs[picks - 1 + len(outs) :]
        out_ref, refs = refs[0], refs[1:]
        grad_refs, refs = refs[:slots], refs[slots:]
        zero_refs, refs = refs[:fresh], refs[fresh:]
        s_ref, acc_k, acc_v, k_t, v_t, k_all, v_all = refs[:7]
        key_refs = [first_k] + [ref.at[0] for ref in arrived_refs] + [own_k]
        value_refs = [first_v] + [ref.at[1] for ref in arrived_refs] + [own_v]
        spans = [slice(slot * block, (slot + 1) * block) for slot in range(slots)]
        step = pl.program_id(0)
        clears = []
        if fresh:
            blank, blank_sem = refs[7:]
            for which, target in enumerate(zero_refs):
                for part in range(clear_steps):
                    place = target.at[pl.ds(part * clear_rows, clear_rows)]
                    slot = blank_sem.at[which * clear_steps + part]
                    clears.append(pltpu.make_async_copy(blank, place, slot))

        @pl.when(step == 0)
        def _():
            if fresh:
                blank[...] = jnp.zeros_like(blank)
            for clear in clears:
                clear.start()
            acc_k[...] = jnp.zeros_like(acc_k)
            acc_v[...] = jnp.zeros_like(acc_v)
            for slot in range(slots):
                k_all[spans[slot]] = key_refs[slot][...]
                v_all[spans[slot]] = value_refs[slot][...]
                k_t[:, spans[slot]] = key_refs[slot][...].T
                v_t[:, spans[slot]] = value_refs[slot][...].T

        q = queries_ref[:, 0].reshape(block, HEAD_DIM)
        g = queries_ref[:, 1].reshape(block, HEAD_DIM)
        top = jnp.full((1, block), MASKED, jnp.float32)
        for part_slots in parts:
            start = part_slots[0] * block
            rows_of = slice(start, (part_slots[-1] + 1) * block)
            scores = dot(k_all[rows_of], q, ROWS_ROWS) * (scale * log2e)
            for slot in part_slots:
                s = scores[slot * block - start : (slot + 1) * block - start]
                if slot == picks:
                    key_pos = lax.broadcasted_iota(jnp.int32, (block, block), 0)
                    query_pos = lax.broadcasted_iota(jnp.int32, (block, block), 1)
                    s = jnp.where(key_pos <= query_pos, s, MASKED)
                s_ref[spans[slot]] = s
                slot_top = jnp.max(s, axis=0, keepdims=True)
                if slot < picks:
                    slot_top = jnp.where(chosen_ref[0, slot] >= 0, slot_top, MASKED)
                top = jnp.maximum(top, slot_top)
        total = jnp.zeros((1, block), jnp.float32)
        for slot in range(slots):
            level = top if slot == picks else jnp.where(chosen_ref[0, slot] >= 0, top, -MASKED)
            e = jnp.exp2(s_ref[spans[slot]] - level)
            s_ref[spans[slot]] = e
            total = total + jnp.sum(e, axis=0, keepdims=True)
        inverse = 1.0 / total
        o_t = jnp.zeros((HEAD_DIM, block), jnp.float32)
        for part_slots in parts:
            rows_of = slice(part_slots[0] * block, (part_slots[-1] + 1) * block)
            w = s_ref[rows_of] * inverse
            s_ref[rows_of] = w
            low = w.astype(jnp.bfloat16)
            o_t = o_t + dot(v_t[:, rows_of], low, ROWS_COLS)
            acc_v[rows_of] += dot(low, g, ROWS_COLS)
        o_t = o_t.astype(jnp.bfloat16).astype(jnp.float32)
        delta = jnp.sum(g.T.astype(jnp.float32) * o_t, axis=0, keepdims=True)
        q_t = jnp.zeros((HEAD_DIM, block), jnp.float32)
        for part_slots in parts:
            rows_of = slice(part_slots[0] * block, (part_slots[-1] + 1) * block)
            w_grad = dot(v_all[rows_of], g, ROWS_ROWS)
            s_grad = (s_ref[rows_of] * (w_grad - delta)).astype(jnp.bfloat16)
            q_t = q_t + dot(k_t[:, rows_of], s_grad, ROWS_COLS)
            acc_k[rows_of] += dot(s_grad, q, ROWS_COLS)
        o = o_t.T.astype(jnp.bfloat16)
        q_grad = (q_t * scale).T.astype(jnp.bfloat16)
        out_ref[:, 0] = o.reshape(count, rows, HEAD_DIM)
        out_ref[:, 1] = q_grad.reshape(count, rows, HEAD_DIM)

        @pl.when(step == group - 1)
        def _():
            for slot in range(slots):
                grad_refs[slot][0] = (acc_k[spans[slot]] * scale).astype(jnp.bfloat16)
                grad_refs[slot][1] = acc_v[spans[slot]].astype(jnp.bfloat16)
            for clear in clears:
                clear.wait()

    def first_index(step, chosen, pos):
        return (jnp.maximum(lax.rem(chosen[0, 0], shard_blocks), 0), head)

    def own_index(step, chosen, pos):
        return (pos[0], head)

    def whole_index(step, chosen, pos):
        return (0, 0, 0)

    piece = pl.BlockSpec((count, 2, rows, HEAD_DIM), lambda step, chosen, pos: (0, head, 0, step))
    pair = pl.BlockSpec((2, block, HEAD_DIM), whole_index)
    flops = 12 * block * slots * block * HEAD_DIM * group
    result = pl.pallas_call(
        kernel,
        grid_spec=pltpu.PrefetchScalarGridSpec(
            num_scalar_prefetch=2,
            grid=(group,),
            in_specs=[piece]
            + [pl.BlockSpec((block, HEAD_DIM), first_index)] * 2
            + [pl.BlockSpec((block, HEAD_DIM), own_index)] * 2
            + [pair] * (picks - 1)
            + [HBM] * len(outs),
            out_specs=[piece] + [pair] * slots + [HBM] * fresh,
            scratch_shapes=[
                pltpu.VMEM((slots * block, block), jnp.float32),
                pltpu.VMEM((slots * block, HEAD_DIM), jnp.float32),
                pltpu.VMEM((slots * block, HEAD_DIM), jnp.float32),
                pltpu.VMEM((HEAD_DIM, slots * block), jnp.bfloat16),
                pltpu.VMEM((HEAD_DIM, slots * block), jnp.bfloat16),
                pltpu.VMEM((slots * block, HEAD_DIM), jnp.bfloat16),
                pltpu.VMEM((slots * block, HEAD_DIM), jnp.bfloat16),
            ]
            + clear_scratch,
        ),
        out_shape=[jax.ShapeDtypeStruct(queries.shape, jnp.bfloat16)]
        + [jax.ShapeDtypeStruct((2, block, HEAD_DIM), jnp.bfloat16)] * slots
        + [jax.ShapeDtypeStruct(keys.shape, keys.dtype)] * fresh,
        compiler_params=pltpu.CompilerParams(vmem_limit_bytes=VMEM_LIMIT),
        cost_estimate=pl.CostEstimate(
            flops=flops, bytes_accessed=8 << 20, transcendentals=block * block * slots * group
        ),
        input_output_aliases={2 + 5 + picks - 1 + i: i for i in range(len(outs))},
        name="attend",
    )(chosen, span_pos, queries, keys, values, keys, values, *arrived, *outs)
    return (result[0], result[1 : 1 + slots], result[1 + slots :])


def finish(seq_index, chosen, span_pos, wanted, outs, contributions, buffers, shapes, head):
    slots = len(contributions)
    picks = slots - 1
    block = contributions[0].shape[1]
    shapes = shapes if outs else shapes[2:]

    def kernel(seq_ref, chosen_ref, pos_ref, *refs):
        wanted_refs, refs = refs[: picks - 1], refs[picks - 1 :]
        out_refs, refs = refs[: len(outs)], refs[len(outs) :]
        given, refs = refs[:slots], refs[slots:]
        refs = refs[len(buffers) :]
        row_refs, refs = refs[: len(shapes) - 2], refs[len(shapes) - 2 :]
        key_ref, value_ref, held, held_rows, sums, read_sem, row_sem, out_sem, grad_sem = refs
        seq = seq_ref[0]
        shard_blocks = key_ref.shape[0] // block
        copies, row_reads = [], []
        for out_ref in out_refs:
            devices, rows, _, part = out_ref.shape
            row_reads.append(pltpu.make_async_copy(out_ref, held_rows, row_sem))
            for place in range(devices * rows // 2):
                device, head_of = place // (rows // 2), place % (rows // 2)
                for which, target in enumerate(row_refs):
                    slot = place * 2 + which
                    piece = (device, head_of * 2 + which)
                    columns = target.at[:, pl.ds(place * part, part)]
                    middle = held_rows.at[piece]
                    copies.append(pltpu.make_async_copy(middle, columns, out_sem.at[slot]))
        reads = [
            pltpu.make_async_copy(given[i], held.at[i], read_sem.at[i]) for i in range(slots)
        ]
        for read in reads + row_reads:
            read.start()
        targets = [jnp.where(chosen_ref[0, 0] >= 0, chosen_ref[0, 0] - seq * shard_blocks, -1)]
        for d in range(1, picks):
            above = seq + d < lax.axis_size("seq")
            local = wanted_refs[d - 1][0, d] - seq * shard_blocks
            targets.append(jnp.where(above, local, -1))
        targets.append(pos_ref[0])
        present = [(t >= 0) & (t < shard_blocks) for t in targets]
        same = {}
        for i in range(slots):
            for j in range(i + 1, slots):
                same[i, j] = present[i] & (targets[i] == targets[j])

        def moves(i, source):
            start = pl.multiple_of(jnp.clip(targets[i], 0, shard_blocks - 1) * block, block)
            place = (pl.ds(start, block), pl.ds(head * HEAD_DIM, HEAD_DIM))
            return [
                pltpu.make_async_copy(source.at[which], target.at[place], grad_sem.at[i * 2 + which])
                for which, target in enumerate((key_ref, value_ref))
            ]

        leads = []
        for read in reads:
            read.wait()
        for i in range(slots):
            lead = present[i]
            for j in range(i):
                lead = lead & jnp.logical_not(same[j, i])
            shared = jnp.bool_(False)
            for j in range(i + 1, slots):
                shared = shared | same[i, j]
            leads.append(lead)

            @pl.when(lead & jnp.logical_not(shared))
            def _(i=i):
                for copy in moves(i, held.at[i]):
                    copy.start()

            @pl.when(lead & shared)
            def _(i=i):
                value = held[i].astype(jnp.float32)
                for j in range(i + 1, slots):
                    value = value + jnp.where(same[i, j], held[j].astype(jnp.float32), 0.0)
                sums[i] = value.astype(jnp.bfloat16)
                for copy in moves(i, sums.at[i]):
                    copy.start()

        for read in row_reads:
            read.wait()
        for copy in copies:
            copy.start()
        for i in range(slots):

            @pl.when(leads[i])
            def _(i=i):
                for copy in moves(i, held.at[i]):
                    copy.wait()

        for copy in copies:
            copy.wait()

    out_copies = outs[0].shape[0] * outs[0].shape[1] if outs else 1
    base = 3 + picks - 1 + len(outs) + slots
    return pl.pallas_call(
        kernel,
        in_specs=[SMEM] * (3 + picks - 1)
        + [HBM] * (len(outs) + slots + len(buffers)),
        out_specs=[HBM] * len(shapes),
        out_shape=shapes,
        scratch_shapes=[
            pltpu.VMEM((slots, 2, block, HEAD_DIM), jnp.bfloat16),
            pltpu.VMEM(outs[0].shape if outs else (16, HEAD_DIM), jnp.bfloat16),
            pltpu.VMEM((slots, 2, block, HEAD_DIM), jnp.bfloat16),
            pltpu.SemaphoreType.DMA((slots,)),
            pltpu.SemaphoreType.DMA,
            pltpu.SemaphoreType.DMA((out_copies,)),
            pltpu.SemaphoreType.DMA((slots * 2,)),
        ],
        input_output_aliases={base + i: len(shapes) - 2 + i for i in range(2)},
        compiler_params=pltpu.CompilerParams(vmem_limit_bytes=VMEM_LIMIT),
        name="finish",
    )(seq_index, chosen, span_pos, *wanted, *outs, *contributions, *buffers)


def per_device(query, keys, values, out_grad, span_pos, selected):
    seq_index = lax.axis_index("seq").astype(jnp.int32).reshape(1)
    heads = keys.shape[1] // HEAD_DIM
    distances = range(1, selected.shape[1])

    wanted = [shifted(selected, "seq", -d) for d in distances]
    queries, outgoing = prepare(query, out_grad, keys, values, wanted, seq_index, heads)
    queries = exchanged(queries, "head")
    arrived = [[shifted(piece[d - 1], "seq", d) for d in distances] for piece in outgoing]
    shapes = [jax.ShapeDtypeStruct(query.shape, query.dtype)] * 2
    shapes += [jax.ShapeDtypeStruct(keys.shape, keys.dtype)] * 2
    buffers, outs, results = [], [], []
    for head in range(heads):
        out, grads, cleared = attend(
            selected, span_pos, queries, keys, values, arrived[head], outs, head
        )
        buffers += cleared
        if results:
            out, grads, results[-1] = lax.optimization_barrier((out, grads, results[-1]))
        outs = [out]
        returned = [shifted(grads[d], "seq", -d) for d in distances]
        results.append([grads[0]] + returned + [grads[-1]])
    out = exchanged(outs[0], "head")
    for head in range(heads):
        given = [out] if head == heads - 1 else []
        buffers = finish(
            seq_index, selected, span_pos, wanted, given, results[head], buffers, shapes, head
        )
    return tuple(buffers)


def solution(mesh):
    in_specs = (
        P(("seq", "head"), None),
        P("seq", "head"),
        P("seq", "head"),
        P(("seq", "head"), None),
        P("seq"),
        P("seq", None),
    )
    out_specs = (
        P(("seq", "head"), None),
        P(("seq", "head"), None),
        P("seq", "head"),
        P("seq", "head"),
    )
    return jax.shard_map(
        per_device, mesh=mesh, in_specs=in_specs, out_specs=out_specs, check_vma=False
    )
```
